32 devices in a mesh: groups: 2 (over x), out: 8 (over z, y), in: 2 (over core).
Axes of the slice: x: 2, y: 2, z: 4, core: 2. Of those that a mesh axis runs over, the one named last changes fastest.
Arguments:
- features: bfloat16 [512, 16384], P(('groups', 'out'), 'in'), parts along dimension 0, may hold values from -6 to 6
- weight: bfloat16 [16384, 16384], P('in', 'out'), may hold values from -0.046875 to 0.046875
- grad_output: bfloat16 [512, 16384], P(('groups', 'in'), 'out'), parts along dimension 0, may hold values from -0.375 to 0.375
Outputs:
- activation: bfloat16 [512, 16384], P(('groups', 'in'), 'out'), parts along dimension 0
- grad_input: bfloat16 [512, 16384], P(('groups', 'out'), 'in'), parts along dimension 0
- grad_weight: bfloat16 [32768, 16384], P(('groups', 'in'), 'out'), parts along dimension 0
The draws below stay inside these ranges and needn't reach their ends.
There are 2 independent parts, one for each index of `groups`. The reference program is written for one: setup_inputs(seed, part) draws one part's arguments, and reference() takes and returns one part's arrays. A program takes and returns all parts, laid end to end along the dimension named above; an argument that names none is the same for every part. Nothing has to cross between parts.
All inputs are finite; a program needn't handle non-finite values.
Results may differ from the reference program's by a relative error of at most 0.005.
Values may be sent and summed in bfloat16 or wider, within the bound.
A program may use at most 192 MiB of HBM per device.

```python
import jax
import jax.numpy as jnp

DIN = 16384
DOUT = 16384
BATCH = 256


def steps_of(stream_key, dims, cuts, low, top_value):
    gain = 1.0
    for position, parts in cuts:
        steps = jax.random.uniform(jax.random.fold_in(jax.random.fold_in(stream_key, 6), position), (parts,), jnp.float32, low / len(cuts), top_value / len(cuts))
        gain = gain * jnp.repeat(jnp.exp(steps), dims[position] // parts).reshape((-1,) + (1,) * (len(dims) - 1 - position))
    return gain


def scatter_about(rng, dims, width, bound, pieces=(), held_as=jnp.bfloat16):
    factor_of = steps_of(rng, dims, pieces, -0.22, 0.18) if pieces else 1.0
    result = jax.random.normal(rng, dims, jnp.float32) * width * factor_of
    return jnp.minimum(jnp.maximum(result, -bound), bound).astype(held_as)


def setup_inputs(seed: int = 0, part: int = 0) -> dict:
    key_of = jax.random.split(jax.random.key(seed), 4)
    part_splits = jax.random.split(jax.random.fold_in(key_of[3], part), 4)
    features = scatter_about(part_splits[0], (BATCH, DIN), 1.0, 6.0, ((0, 8), (1, 2)))
    weight = scatter_about(key_of[1], (DIN, DOUT), DIN ** -0.5, 0.046875, ((0, 2), (1, 8)))
    grad_output = scatter_about(part_splits[2], (BATCH, DOUT), (BATCH ** -0.5), 0.375, ((0, 2), (1, 8)))
    return {"features": features, "weight": weight, "grad_output": grad_output}


def reference(features, weight, grad_output):
    pre = jnp.dot(features, weight, preferred_element_type=jnp.float32)
    sig = jax.nn.sigmoid(pre)
    activation = (pre * sig).astype(jnp.bfloat16)
    grad_pre = (grad_output.astype(jnp.float32) * sig * (1.0 + pre * (1.0 - sig))).astype(jnp.bfloat16)
    grad_input = jnp.dot(grad_pre, weight.T, preferred_element_type=jnp.float32).astype(jnp.bfloat16)
    grad_weight = jnp.dot(features.T, grad_pre, preferred_element_type=jnp.float32).astype(jnp.bfloat16)
    return activation, grad_input, grad_weight
```

```python
import functools

import jax
import jax.numpy as jnp
from jax import lax
from jax.experimental import pallas as pl
from jax.experimental.pallas import tpu as pltpu
from jax.sharding import PartitionSpec as P

MESH = pl.DeviceIdType.MESH
CHUNKS = 8
F32 = jnp.float32
BF16 = jnp.bfloat16


def layer_kernel(
    nz, ny, chunks,
    x_ref, w_ref, g_ref,
    act_ref, gi_ref, xall_out, gp_out,
    xall, w, acc, theirs, gp, keep, ysend, yrecv, zsend, zrecv,
    w_sem, x_sem, out_sem,
    zs, zr, ys, yr, ps, pr, gs, gr, rys, ryr, rzs, rzr,
):
    n, rows, depth = xall.shape
    width = w.shape[1]
    batch = n * rows
    half = batch // 2
    cc = depth // chunks
    nt = min(512, width)
    tiles = width // nt
    me = lax.axis_index("out")
    z, y = me // ny, lax.rem(me, ny)
    core = lax.axis_index("in")
    other_y = z * ny + (1 - y)
    other_core = 1 - core

    def ahead(d):
        return lax.rem(z + d, nz)

    def behind(d):
        return lax.rem(z + nz - d, nz)

    def cols(k):
        return pl.ds(pl.multiple_of(k * cc, cc), cc)

    def tile(j):
        return pl.ds(pl.multiple_of(j * nt, nt), nt)

    def to_out(src, dst, send, recv, peer):
        return pltpu.make_async_remote_copy(
            src_ref=src, dst_ref=dst, send_sem=send, recv_sem=recv,
            device_id={"out": peer}, device_id_type=MESH)

    def to_core(src, dst, send, recv):
        return pltpu.make_async_remote_copy(
            src_ref=src, dst_ref=dst, send_sem=send, recv_sem=recv,
            device_id={"in": other_core}, device_id_type=MESH)

    def w_copy(k):
        return pltpu.make_async_copy(w_ref.at[cols(k), :], w.at[cols(k), :], w_sem.at[k])

    own_copy = pltpu.make_async_copy(x_ref, xall.at[me], x_sem.at[0])
    own_copy.start()

    barrier = pltpu.get_barrier_semaphore()
    for d in range(1, nz):
        pl.semaphore_signal(barrier, inc=1, device_id={"out": ahead(d) * ny + y}, device_id_type=MESH)
    pl.semaphore_signal(barrier, inc=1, device_id={"out": other_y}, device_id_type=MESH)
    pl.semaphore_signal(barrier, inc=1, device_id={"in": other_core}, device_id_type=MESH)
    pl.semaphore_wait(barrier, nz + 1)

    def z_copy(k, d, slot):
        return to_out(x_ref.at[:, cols(k)], xall.at[slot, :, cols(k)], zs.at[k, d - 1], zr.at[k, d - 1], ahead(d) * ny + y)

    def y_own(k, slot):
        return to_out(x_ref.at[:, cols(k)], xall.at[slot, :, cols(k)], ys.at[k, 0], yr.at[k, 0], other_y)

    def y_pass(k, d, slot):
        return to_out(xall.at[slot, :, cols(k)], xall.at[slot, :, cols(k)], ys.at[k, d], yr.at[k, d], other_y)

    @pl.loop(0, chunks)
    def _(k):
        for d in range(1, nz):
            z_copy(k, d, me).start()
        y_own(k, me).start()

    @pl.loop(0, chunks)
    def _(k):
        w_copy(k).start()

    acc[...] = jnp.zeros_like(acc)
    own_copy.wait()

    def forward(k):
        for d in range(1, nz):
            slot = behind(d) * ny + y
            z_copy(k, d, slot).wait_recv()
            y_pass(k, d, slot).start()

    def arrive(k):
        y_own(k, other_y).wait_recv()
        for d in range(1, nz):
            y_pass(k, d, behind(d) * ny + (1 - y)).wait_recv()
        w_copy(k).wait()

    def multiply(k, j):
        acc[:, tile(j)] += jnp.dot(
            xall[:, :, cols(k)].reshape(batch, cc), w[cols(k), tile(j)], preferred_element_type=F32)

    forward(0)

    @pl.loop(1, chunks)
    def _(k):
        forward(k)
        arrive(k - 1)

        @pl.loop(0, tiles)
        def _(j):
            multiply(k - 1, j)

    own_rows = pl.ds(pl.multiple_of(core * half, half), half)
    other_rows = pl.ds(pl.multiple_of(other_core * half, half), half)

    def pre_copy(j):
        return to_core(acc.at[other_rows, tile(j)], theirs.at[:, tile(j)], ps.at[j], pr.at[j])

    def gp_copy(j, where):
        return to_core(gp.at[where, tile(j)], gp.at[where, tile(j)], gs.at[j], gr.at[j])

    arrive(chunks - 1)

    @pl.loop(0, tiles)
    def _(j):
        multiply(chunks - 1, j)
        pre_copy(j).start()

    xall_copy = pltpu.make_async_copy(xall, xall_out, out_sem.at[0])
    xall_copy.start()

    @pl.loop(0, tiles)
    def _(j):
        pre_copy(j).wait_recv()
        pre = acc[own_rows, tile(j)] + theirs[:, tile(j)]
        sig = 1.0 / (1.0 + jnp.exp(-pre))
        act_ref[:, tile(j)] = (pre * sig).astype(BF16)
        gp[own_rows, tile(j)] = (g_ref[:, tile(j)].astype(F32) * sig * (1.0 + pre * (1.0 - sig))).astype(BF16)
        gp_copy(j, own_rows).start()

    @pl.loop(0, tiles)
    def _(j):
        gp_copy(j, other_rows).wait_recv()

    gp_out_copy = pltpu.make_async_copy(gp, gp_out, out_sem.at[1])
    gp_out_copy.start()

    def y_sum(k):
        return to_out(ysend.at[:, :, cols(k)], yrecv.at[:, :, cols(k)], rys.at[k], ryr.at[k], other_y)

    def z_sum(k, d):
        return to_out(zsend.at[ahead(d), :, cols(k)], zrecv.at[d - 1, :, cols(k)], rzs.at[k, d - 1], rzr.at[k, d - 1], ahead(d) * ny + y)

    step = min(512, cc)

    def partial(k):
        @pl.loop(0, cc // step)
        def _(i):
            at = pl.ds(pl.multiple_of(k * cc + i * step, step), step)
            part = lax.dot_general(
                gp[...], w[at, :], (((1,), (1,)), ((), ())), preferred_element_type=F32
            ).reshape(nz, ny, rows, step)
            keep[:, :, at] = jnp.where(y == 0, part[:, 0], part[:, 1])
            ysend[:, :, at] = jnp.where(y == 0, part[:, 1], part[:, 0]).astype(BF16)

        y_sum(k).start()

    def combine(k):
        y_sum(k).wait_recv()
        total = keep[:, :, cols(k)] + yrecv[:, :, cols(k)].astype(F32)
        keep[:, :, cols(k)] = total
        zsend[:, :, cols(k)] = total.astype(BF16)
        for d in range(1, nz):
            z_sum(k, d).start()

    def finish(k):
        total = keep[z, :, cols(k)]
        for d in range(1, nz):
            z_sum(k, d).wait_recv()
            total = total + zrecv[d - 1, :, cols(k)].astype(F32)
        gi_ref[:, cols(k)] = total.astype(BF16)

    @pl.loop(0, chunks + 2)
    def _(k):
        @pl.when(k < chunks)
        def _():
            partial(k)

        @pl.when(k >= 2)
        def _():
            combine(k - 2)

    @pl.loop(0, chunks)
    def _(k):
        finish(k)

    @pl.loop(0, chunks)
    def _(k):
        for d in range(1, nz):
            z_copy(k, d, me).wait_send()
            y_pass(k, d, behind(d) * ny + y).wait_send()
            z_sum(k, d).wait_send()
        y_own(k, me).wait_send()
        y_sum(k).wait_send()

    @pl.loop(0, tiles)
    def _(j):
        pre_copy(j).wait_send()
        gp_copy(j, own_rows).wait_send()

    xall_copy.wait()
    gp_out_copy.wait()


def outer_kernel(x_ref, gp_ref, out_ref):
    width = gp_ref.shape[1]
    nt = min(512, width)

    @pl.loop(0, width // nt)
    def _(j):
        at = pl.ds(pl.multiple_of(j * nt, nt), nt)
        out_ref[:, at] = lax.dot_general(
            x_ref[...], gp_ref[:, at], (((0,), (0,)), ((), ())), preferred_element_type=F32
        ).astype(BF16)


def solution(mesh):
    n = mesh.shape["out"]
    ny = 2
    nz = n // ny

    def shards(features, weight, grad_output):
        rows, depth = features.shape
        width = weight.shape[1]
        batch = n * rows
        half = batch // 2
        chunks = CHUNKS
        tiles = width // min(512, width)
        dma = pltpu.SemaphoreType.DMA
        hbm = pl.BlockSpec(memory_space=pl.ANY)
        vmem = pl.BlockSpec(memory_space=pltpu.VMEM)
        activation, grad_input, all_inputs, grad_pre = pl.pallas_call(
            functools.partial(layer_kernel, nz, ny, chunks),
            out_shape=(
                jax.ShapeDtypeStruct((half, width), BF16),
                jax.ShapeDtypeStruct((rows, depth), BF16),
                jax.ShapeDtypeStruct((n, rows, depth), BF16),
                jax.ShapeDtypeStruct((batch, width), BF16),
            ),
            in_specs=[hbm, hbm, vmem],
            out_specs=(vmem, vmem, hbm, hbm),
            scratch_shapes=[
                pltpu.VMEM((n, rows, depth), BF16),
                pltpu.VMEM((depth, width), BF16),
                pltpu.VMEM((batch, width), F32),
                pltpu.VMEM((half, width), F32),
                pltpu.VMEM((batch, width), BF16),
                pltpu.VMEM((nz, rows, depth), F32),
                pltpu.VMEM((nz, rows, depth), BF16),
                pltpu.VMEM((nz, rows, depth), BF16),
                pltpu.VMEM((nz, rows, depth), BF16),
                pltpu.VMEM((nz - 1, rows, depth), BF16),
                dma((chunks,)), dma((1,)), dma((2,)),
                dma((chunks, nz - 1)), dma((chunks, nz - 1)),
                dma((chunks, nz)), dma((chunks, nz)),
                dma((tiles,)), dma((tiles,)), dma((tiles,)), dma((tiles,)),
                dma((chunks,)), dma((chunks,)),
                dma((chunks, nz - 1)), dma((chunks, nz - 1)),
            ],
            compiler_params=pltpu.CompilerParams(
                collective_id=0, has_side_effects=True, vmem_limit_bytes=62 * 2**20),
            cost_estimate=pl.CostEstimate(
                flops=4 * batch * depth * width, bytes_accessed=2 * depth * width, transcendentals=half * width),
            name="layer",
        )(features, weight, grad_output)
        block = min(512, depth)
        grad_weight = pl.pallas_call(
            outer_kernel,
            out_shape=jax.ShapeDtypeStruct((depth, width), BF16),
            grid=(depth // block,),
            in_specs=[
                pl.BlockSpec((batch, block), lambda i: (0, i)),
                pl.BlockSpec((batch, width), lambda i: (0, 0)),
            ],
            out_specs=pl.BlockSpec((block, width), lambda i: (i, 0)),
            compiler_params=pltpu.CompilerParams(vmem_limit_bytes=40 * 2**20),
            cost_estimate=pl.CostEstimate(
                flops=2 * batch * depth * width, bytes_accessed=2 * depth * width, transcendentals=0),
            name="outer",
        )(all_inputs.reshape(batch, depth), grad_pre)
        return activation, grad_input, grad_weight

    in_specs = (P(("groups", "out"), "in"), P("in", "out"), P(("groups", "in"), "out"))
    out_specs = (P(("groups", "in"), "out"), P(("groups", "out"), "in"), P(("groups", "in"), "out"))
    return jax.shard_map(shards, mesh=mesh, in_specs=in_specs, out_specs=out_specs, check_vma=False)
```

```python
import functools

import jax
import jax.numpy as jnp
from jax import lax
from jax.experimental import pallas as pl
from jax.experimental.pallas import tpu as pltpu
from jax.sharding import PartitionSpec as P

MESH = pl.DeviceIdType.MESH
CHUNKS = 8
AHEAD = 2
F32 = jnp.float32
BF16 = jnp.bfloat16


def layer_kernel(
    nz, ny, chunks,
    x_ref, w_ref, g_ref,
    act_ref, gi_ref, xt_out, gp_out,
    xall, xt, w, acc, theirs, gp, keep, ysend, yrecv, zsend, zrecv,
    w_sem, x_sem, out_sem,
    zs, zr, ys, yr, ps, pr, gs, gr, rys, ryr, rzs, rzr,
):
    n, rows, depth = xall.shape
    width = w.shape[1]
    batch = n * rows
    half = batch // 2
    cc = depth // chunks
    nt = min(512, width)
    tiles = width // nt
    me = lax.axis_index("out")
    z, y = me // ny, lax.rem(me, ny)
    core = lax.axis_index("in")
    other_y = z * ny + (1 - y)
    other_core = 1 - core

    def ahead(d):
        return lax.rem(z + d, nz)

    def behind(d):
        return lax.rem(z + nz - d, nz)

    def cols(k):
        return pl.ds(pl.multiple_of(k * cc, cc), cc)

    def tile(j):
        return pl.ds(pl.multiple_of(j * nt, nt), nt)

    def to_out(src, dst, send, recv, peer):
        return pltpu.make_async_remote_copy(
            src_ref=src, dst_ref=dst, send_sem=send, recv_sem=recv,
            device_id={"out": peer}, device_id_type=MESH)

    def to_core(src, dst, send, recv):
        return pltpu.make_async_remote_copy(
            src_ref=src, dst_ref=dst, send_sem=send, recv_sem=recv,
            device_id={"in": other_core}, device_id_type=MESH)

    def w_copy(k):
        return pltpu.make_async_copy(w_ref.at[cols(k), :], w.at[cols(k), :], w_sem.at[k])

    own_copy = pltpu.make_async_copy(x_ref, xall.at[me], x_sem.at[0])
    own_copy.start()

    barrier = pltpu.get_barrier_semaphore()
    for d in range(1, nz):
        pl.semaphore_signal(barrier, inc=1, device_id={"out": ahead(d) * ny + y}, device_id_type=MESH)
    pl.semaphore_signal(barrier, inc=1, device_id={"out": other_y}, device_id_type=MESH)
    pl.semaphore_signal(barrier, inc=1, device_id={"in": other_core}, device_id_type=MESH)
    pl.semaphore_wait(barrier, nz + 1)

    def z_copy(k, d, slot):
        return to_out(x_ref.at[:, cols(k)], xall.at[slot, :, cols(k)], zs.at[k, d - 1], zr.at[k, d - 1], ahead(d) * ny + y)

    def y_own(k, slot):
        return to_out(x_ref.at[:, cols(k)], xall.at[slot, :, cols(k)], ys.at[k, 0], yr.at[k, 0], other_y)

    def y_pass(k, d, slot):
        return to_out(xall.at[slot, :, cols(k)], xall.at[slot, :, cols(k)], ys.at[k, d], yr.at[k, d], other_y)

    def send(k):
        for d in range(1, nz):
            z_copy(k, d, me).start()
        y_own(k, me).start()

    @pl.loop(0, AHEAD)
    def _(k):
        send(k)

    @pl.loop(0, chunks)
    def _(k):
        w_copy(k).start()

    acc[...] = jnp.zeros_like(acc)
    own_copy.wait()

    def forward(k):
        for d in range(1, nz):
            slot = behind(d) * ny + y
            z_copy(k, d, slot).wait_recv()
            y_pass(k, d, slot).start()

        @pl.when(k + AHEAD < chunks)
        def _():
            send(k + AHEAD)

    def arrive(k):
        y_own(k, other_y).wait_recv()
        for d in range(1, nz):
            y_pass(k, d, behind(d) * ny + (1 - y)).wait_recv()
        w_copy(k).wait()

    def xt_copy(k):
        slot = lax.rem(k, 2)
        return pltpu.make_async_copy(xt.at[slot], xt_out.at[cols(k), :], out_sem.at[slot])

    strip = min(256, cc)

    def turn(k):
        slot = lax.rem(k, 2)

        @pl.when(k >= 2)
        def _():
            xt_copy(k - 2).wait()

        @pl.loop(0, cc // strip)
        def _(i):
            at = pl.multiple_of(i * strip, strip)
            block = xall[:, :, pl.ds(pl.multiple_of(k * cc + at, strip), strip)]
            xt[slot, pl.ds(at, strip), :] = block.reshape(batch, strip).T

        xt_copy(k).start()

    def multiply(k, j):
        acc[:, tile(j)] += jnp.dot(
            xall[:, :, cols(k)].reshape(batch, cc), w[cols(k), tile(j)], preferred_element_type=F32)

    forward(jnp.int32(0))

    @pl.loop(1, chunks)
    def _(k):
        forward(k)
        arrive(k - 1)

        @pl.loop(0, tiles)
        def _(j):
            multiply(k - 1, j)

        turn(k - 1)

    own_rows = pl.ds(pl.multiple_of(core * half, half), half)
    other_rows = pl.ds(pl.multiple_of(other_core * half, half), half)

    def pre_copy(j):
        return to_core(acc.at[other_rows, tile(j)], theirs.at[:, tile(j)], ps.at[j], pr.at[j])

    def gp_copy(j, where):
        return to_core(gp.at[where, tile(j)], gp.at[where, tile(j)], gs.at[j], gr.at[j])

    arrive(chunks - 1)

    @pl.loop(0, tiles)
    def _(j):
        multiply(chunks - 1, j)
        pre_copy(j).start()

    turn(jnp.int32(chunks - 1))

    @pl.loop(0, tiles)
    def _(j):
        pre_copy(j).wait_recv()
        pre = acc[own_rows, tile(j)] + theirs[:, tile(j)]
        sig = 1.0 / (1.0 + jnp.exp(-pre))
        act_ref[:, tile(j)] = (pre * sig).astype(BF16)
        gp[own_rows, tile(j)] = (g_ref[:, tile(j)].astype(F32) * sig * (1.0 + pre * (1.0 - sig))).astype(BF16)
        gp_copy(j, own_rows).start()

    @pl.loop(0, tiles)
    def _(j):
        gp_copy(j, other_rows).wait_recv()

    gp_out_copy = pltpu.make_async_copy(gp, gp_out, out_sem.at[2])
    gp_out_copy.start()

    def y_sum(k):
        return to_out(ysend.at[:, :, cols(k)], yrecv.at[:, :, cols(k)], rys.at[k], ryr.at[k], other_y)

    def z_sum(k, d):
        return to_out(zsend.at[ahead(d), :, cols(k)], zrecv.at[d - 1, :, cols(k)], rzs.at[k, d - 1], rzr.at[k, d - 1], ahead(d) * ny + y)

    step = min(512, cc)

    def partial(k):
        @pl.loop(0, cc // step)
        def _(i):
            at = pl.ds(pl.multiple_of(k * cc + i * step, step), step)
            part = lax.dot_general(
                gp[...], w[at, :], (((1,), (1,)), ((), ())), preferred_element_type=F32
            ).reshape(nz, ny, rows, step)
            keep[:, :, at] = jnp.where(y == 0, part[:, 0], part[:, 1])
            ysend[:, :, at] = jnp.where(y == 0, part[:, 1], part[:, 0]).astype(BF16)

        y_sum(k).start()

    def combine(k):
        y_sum(k).wait_recv()
        total = keep[:, :, cols(k)] + yrecv[:, :, cols(k)].astype(F32)
        keep[:, :, cols(k)] = total
        zsend[:, :, cols(k)] = total.astype(BF16)
        for d in range(1, nz):
            z_sum(k, d).start()

    def finish(k):
        total = keep[z, :, cols(k)]
        for d in range(1, nz):
            z_sum(k, d).wait_recv()
            total = total + zrecv[d - 1, :, cols(k)].astype(F32)
        gi_ref[:, cols(k)] = total.astype(BF16)

    @pl.loop(0, chunks + 2)
    def _(k):
        @pl.when(k < chunks)
        def _():
            partial(k)

        @pl.when(k >= 2)
        def _():
            combine(k - 2)

    @pl.loop(0, chunks)
    def _(k):
        finish(k)

    @pl.loop(0, chunks)
    def _(k):
        for d in range(1, nz):
            z_copy(k, d, me).wait_send()
            y_pass(k, d, behind(d) * ny + y).wait_send()
            z_sum(k, d).wait_send()
        y_own(k, me).wait_send()
        y_sum(k).wait_send()

    @pl.loop(0, tiles)
    def _(j):
        pre_copy(j).wait_send()
        gp_copy(j, own_rows).wait_send()

    xt_copy(chunks - 2).wait()
    xt_copy(chunks - 1).wait()
    gp_out_copy.wait()


SLOTS = 3
PARTS = 4


def outer_kernel(steps, xt_ref, gp_ref, act_in, gi_in, out_ref, act_ref, gi_ref, held, sems):
    block, width = held.shape[1:]
    nt = min(512, width)
    part = block // PARTS
    i = pl.program_id(0)
    act_ref[...] = act_in[...]
    gi_ref[...] = gi_in[...]

    def copy(i, p):
        slot = lax.rem(i, SLOTS)
        return pltpu.make_async_copy(
            held.at[slot, pl.ds(p * part, part), :],
            out_ref.at[pl.ds(pl.multiple_of(i * block + p * part, part), part), :],
            sems.at[slot, p])

    @pl.when(i >= SLOTS)
    def _():
        for p in range(PARTS):
            copy(i - SLOTS, p).wait()

    slot = lax.rem(i, SLOTS)

    for j in range(width // nt):
        at = pl.ds(j * nt, nt)
        held[slot, :, at] = jnp.dot(xt_ref[...], gp_ref[:, at], preferred_element_type=F32).astype(BF16)

    for p in range(PARTS):
        copy(i, p).start()

    @pl.when(i == steps - 1)
    def _():
        for back in range(min(SLOTS, steps)):
            for p in range(PARTS):
                copy(steps - 1 - back, p).wait()


def solution(mesh):
    n = mesh.shape["out"]
    ny = 2
    nz = n // ny

    def shards(features, weight, grad_output):
        rows, depth = features.shape
        width = weight.shape[1]
        batch = n * rows
        half = batch // 2
        chunks = CHUNKS
        tiles = width // min(512, width)
        dma = pltpu.SemaphoreType.DMA
        hbm = pl.BlockSpec(memory_space=pl.ANY)
        vmem = pl.BlockSpec(memory_space=pltpu.VMEM)
        activation, grad_input, turned, grad_pre = pl.pallas_call(
            functools.partial(layer_kernel, nz, ny, chunks),
            out_shape=(
                jax.ShapeDtypeStruct((half, width), BF16),
                jax.ShapeDtypeStruct((rows, depth), BF16),
                jax.ShapeDtypeStruct((depth, batch), BF16),
                jax.ShapeDtypeStruct((batch, width), BF16),
            ),
            in_specs=[hbm, hbm, vmem],
            out_specs=(vmem, vmem, hbm, hbm),
            scratch_shapes=[
                pltpu.VMEM((n, rows, depth), BF16),
                pltpu.VMEM((2, depth // chunks, batch), BF16),
                pltpu.VMEM((depth, width), BF16),
                pltpu.VMEM((batch, width), F32),
                pltpu.VMEM((half, width), F32),
                pltpu.VMEM((batch, width), BF16),
                pltpu.VMEM((nz, rows, depth), F32),
                pltpu.VMEM((nz, rows, depth), BF16),
                pltpu.VMEM((nz, rows, depth), BF16),
                pltpu.VMEM((nz, rows, depth), BF16),
                pltpu.VMEM((nz - 1, rows, depth), BF16),
                dma((chunks,)), dma((1,)), dma((3,)),
                dma((chunks, nz - 1)), dma((chunks, nz - 1)),
                dma((chunks, nz)), dma((chunks, nz)),
                dma((tiles,)), dma((tiles,)), dma((tiles,)), dma((tiles,)),
                dma((chunks,)), dma((chunks,)),
                dma((chunks, nz - 1)), dma((chunks, nz - 1)),
            ],
            compiler_params=pltpu.CompilerParams(
                collective_id=0, has_side_effects=True, vmem_limit_bytes=62 * 2**20),
            cost_estimate=pl.CostEstimate(
                flops=4 * batch * depth * width, bytes_accessed=2 * depth * width, transcendentals=half * width),
            name="layer",
        )(features, weight, grad_output)
        block = min(1024, depth // 4)
        steps = depth // block
        act_rows = half // min(steps, half // 16)
        act_spec = pl.BlockSpec((act_rows, width), lambda i: (jnp.minimum(i, half // act_rows - 1), 0))
        gi_spec = pl.BlockSpec((rows, block), lambda i: (0, i))
        grad_weight, activation, grad_input = pl.pallas_call(
            functools.partial(outer_kernel, steps),
            out_shape=(
                jax.ShapeDtypeStruct((depth, width), BF16),
                jax.ShapeDtypeStruct((half, width), BF16),
                jax.ShapeDtypeStruct((rows, depth), BF16),
            ),
            grid=(steps,),
            in_specs=[
                pl.BlockSpec((block, batch), lambda i: (i, 0)),
                pl.BlockSpec((batch, width), lambda i: (0, 0)),
                act_spec,
                gi_spec,
            ],
            out_specs=(hbm, act_spec, gi_spec),
            scratch_shapes=[pltpu.VMEM((SLOTS, block, width), BF16), dma((SLOTS, PARTS))],
            compiler_params=pltpu.CompilerParams(vmem_limit_bytes=62 * 2**20),
            cost_estimate=pl.CostEstimate(
                flops=2 * batch * depth * width, bytes_accessed=2 * depth * width, transcendentals=0),
            name="outer",
        )(turned, grad_pre, activation, grad_input)
        return activation, grad_input, grad_weight

    in_specs = (P(("groups", "out"), "in"), P("in", "out"), P(("groups", "in"), "out"))
    out_specs = (P(("groups", "in"), "out"), P(("groups", "out"), "in"), P(("groups", "in"), "out"))
    return jax.shard_map(shards, mesh=mesh, in_specs=in_specs, out_specs=out_specs, check_vma=False)
```
